32 devices in a mesh: expert: 8 (over y, x, core), dp: 4 (over z).
Axes of the slice: x: 2, y: 2, z: 4, core: 2. Of those that a mesh axis runs over, the one named last changes fastest.
Arguments:
- tokens: bfloat16 [512, 1664], P(('expert', 'dp')), may hold values from -6 to 6
- cotangent: bfloat16 [512, 1664], P(('expert', 'dp')), may hold values from -1.1953125 to 1.1953125
- expert_ids: int32 [512, 2], P(('expert', 'dp')), may hold values from 0 to 7, all different within a row; in each aligned block of 16 rows (0 to 15, 16 to 31, ...) at most 8 rows name the same one
- gates: bfloat16 [512, 2], P(('expert', 'dp')), may hold values from 0.099609375 to 1
- w_in: bfloat16 [8, 1664, 4096], P('expert', None, 'dp'), may hold values from -0.15625 to 0.15625
- w_out: bfloat16 [8, 4096, 1664], P('expert', 'dp'), may hold values from -0.09375 to 0.09375
Outputs:
- token_grads: bfloat16 [512, 1664], P(('expert', 'dp'))
- gate_grads: bfloat16 [512, 2], P(('expert', 'dp'))
- grad_in_weights: bfloat16 [8, 1664, 4096], P('expert', None, 'dp')
- grad_out_weights: bfloat16 [8, 4096, 1664], P('expert', 'dp')
The draws below stay inside these ranges and needn't reach their ends.
Inputs may be any that keep to these rules, and one draw needn't show every extreme that they name: `expert_ids`: the two experts of a token differ, and no expert is named by more than 8 of the 16 tokens of one device.
All inputs are finite; a program needn't handle non-finite values.
Results may differ from the reference program's by a relative error of at most 0.019.
Values may be sent and summed in bfloat16 or wider, within the bound.
A program may use at most 64 MiB of HBM per device.

```python
import math
import jax
import jax.numpy as jnp
import numpy as np
from jax import lax

D = 1664
FF = 4096
TOK_DEV = 16
EXPERTS = 8
CAP = 8
TOKENS = 512
N_DP = 4


def shard_levels(stream_key, shape, shards, low, largest):
    gain, own = 1.0, jax.random.fold_in(stream_key, 6)
    for dim, shards_of in shards:
        draws = jnp.exp(jax.random.uniform(jax.random.fold_in(own, dim), (shards_of,), jnp.float32, low / len(shards), largest / len(shards)))
        gain = gain * jnp.repeat(draws, shape[dim] // shards_of).reshape([-1 if axis == dim else 1 for axis in range(len(shape))])
    return gain


def shared_out(stream_key, own, number, rows, amount, top, bound, lean):
    order = jax.random.permutation(stream_key, amount)
    packed, ordinary = portions_of(amount, rows * top, bound, lean, True), portions_of(amount, rows * top, bound, lean, False)
    places = jnp.arange(amount)

    def named(sizes, turn):
        used = int((sizes > 0).sum())
        fixed = max(1, used // 4)
        moved = fixed + (places - fixed + turn * (used - fixed)) % max(1, amount - fixed)
        return jnp.zeros((amount,), jnp.int32).at[order[jnp.where(places < fixed, places, moved)]].set(jnp.asarray(sizes, jnp.int32))

    sizes = jnp.where(number % 4 == 0, named(packed, number // 4), named(ordinary, number - number // 4 - 1))
    mixed = jax.random.permutation(jax.random.fold_in(own, 3), amount)
    donor, taker = mixed[0:amount // 2 * 2:2], mixed[1:amount // 2 * 2:2]
    slack = jnp.minimum(sizes[donor] - 1, bound - sizes[taker]) // 2
    slack = jnp.where((donor == order[0]) | (taker == order[0]) | (sizes[taker] == 0), 0, jnp.maximum(slack, 0))
    moved = jax.random.randint(jax.random.fold_in(own, 4), (amount // 2,), 0, 1 << 20) % (slack + 1)
    sizes = sizes.at[donor].add(-moved).at[taker].add(moved)
    members = jnp.searchsorted(jnp.cumsum(sizes), jnp.arange(rows * top), side="right").astype(jnp.int32)
    listing = members.reshape(top, rows).T
    listing = listing[jax.random.permutation(jax.random.fold_in(own, 1), rows)]
    turn = jax.random.randint(jax.random.fold_in(own, 2), (rows, 1), 0, top)
    return jnp.take_along_axis(listing, (jnp.arange(top)[None, :] + turn) % top, axis=1)


def portions_of(amount, total, most, skew, full):
    loads = [(1 << 20) // math.isqrt(grade ** skew) + 1 for grade in range(1, amount + 1)]
    largest = most if full else min(most, max(-(-total // amount), total * loads[0] // sum(loads)))
    least = 1 if total - largest >= amount - 1 else 0
    holding, spare = [largest] + [least] * (amount - 1), total - largest - least * (amount - 1)
    while spare > 0:
        free = [i for i in range(1, amount) if holding[i] < largest] or [i for i in range(1, amount) if holding[i] < most]
        mass, remaining = sum([loads[i] for i in free]), spare
        for i in free:
            extra = min(most - holding[i], max(1, remaining * loads[i] // mass), spare)
            holding[i] = holding[i] + extra
            spare = spare - extra
    return np.array(holding)


def normal_values(key, dims, width, reach, shards=(), kind=jnp.bfloat16):
    result = width * jax.random.normal(key, dims, jnp.float32)
    if shards:
        result = result * shard_levels(key, dims, shards, -0.22, 0.18)
    return jnp.clip(result, -reach, reach).astype(kind)


def setup_inputs(seed: int = 0) -> dict:
    seeds = jax.random.split(jax.random.key(seed), 7)
    tokens = normal_values(seeds[0], (TOKENS, D), 1.0, 6.0, ((0, 32),))
    cotangent = normal_values(seeds[1], (TOKENS, D), 0.2, 1.1953125, ((0, 32),))
    expert_ids_keys = jax.random.split(jax.random.fold_in(seeds[2], 1), TOKENS // TOK_DEV)
    expert_ids_turns = jax.random.permutation(jax.random.fold_in(seeds[2], 3), TOKENS // TOK_DEV)
    expert_ids = jax.vmap(lambda own, number: shared_out(jax.random.fold_in(seeds[2], 2), own, number, TOK_DEV, EXPERTS, 2, CAP, 2))(expert_ids_keys, expert_ids_turns).reshape((TOKENS, 2))
    gates = jnp.clip(0.099609375 + 0.9003906 * jax.random.uniform(seeds[3], (TOKENS, 2), jnp.float32) ** shard_levels(seeds[3], (TOKENS, 2), ((0, 32),), -0.2, 0.2), 0.099609375, 1.0).astype(jnp.bfloat16)
    w_in = normal_values(seeds[4], (EXPERTS, D, FF), D ** -0.5, 0.15625, ((0, 8), (2, 4)))
    w_out = normal_values(seeds[5], (EXPERTS, FF, D), FF ** -0.5, 0.09375, ((0, 8), (1, 4)))
    return {"tokens": tokens, "cotangent": cotangent, "expert_ids": expert_ids, "gates": gates, "w_in": w_in, "w_out": w_out}


def normal_parts(pre):
    cdf = 0.5 * (1.0 + lax.erf(pre * 0.7071067811865476))
    pdf = 0.3989422804014327 * jnp.exp(-0.5 * pre * pre)
    return cdf, pdf


def reference(tokens, cotangent, expert_ids, gates, w_in, w_out):
    blocks = TOKENS // TOK_DEV
    assign = 2 * TOK_DEV
    rows_per = blocks * CAP
    flat_ids = expert_ids.reshape(blocks, assign).astype(jnp.int32)
    onehot = (flat_ids[:, :, None] == jnp.arange(EXPERTS, dtype=jnp.int32)[None, None, :]).astype(jnp.int32)
    before = (jnp.cumsum(onehot, axis=1) - onehot).astype(jnp.int32)
    slot = jnp.sum(before * onehot, axis=2).astype(jnp.int32)
    block_num = jnp.arange(blocks, dtype=jnp.int32)[:, None]
    index = (flat_ids * rows_per + block_num * CAP + slot).reshape(-1).astype(jnp.int32)
    src_in = jnp.repeat(tokens, 2, axis=0)
    src_cot = jnp.repeat(cotangent, 2, axis=0)
    disp_in = jnp.zeros((EXPERTS * rows_per, D), jnp.bfloat16).at[index].set(src_in).reshape(EXPERTS, rows_per, D)
    disp_cot = jnp.zeros((EXPERTS * rows_per, D), jnp.bfloat16).at[index].set(src_cot).reshape(EXPERTS, rows_per, D)
    disp_gate = jnp.zeros((EXPERTS * rows_per,), jnp.bfloat16).at[index].set(gates.reshape(-1)).reshape(EXPERTS, rows_per)
    group = FF // N_DP

    def expert_step(items):
        x_rows, cot_rows, gate_rows, w_first, w_second = items
        pre = jnp.dot(x_rows, w_first, preferred_element_type=jnp.float32)
        cdf, pdf = normal_parts(pre)
        hidden = (pre * cdf).astype(jnp.bfloat16)
        back = lax.dot_general(cot_rows, w_second, (((1,), (1,)), ((), ())), preferred_element_type=jnp.float32)
        gate_f = gate_rows.astype(jnp.float32)[:, None]
        scaled = (gate_f * cot_rows.astype(jnp.float32)).astype(jnp.bfloat16)
        grad_second = lax.dot_general(hidden, scaled, (((0,), (0,)), ((), ())), preferred_element_type=jnp.float32).astype(jnp.bfloat16)
        pre_grad = (gate_f * back * (cdf + pre * pdf)).astype(jnp.bfloat16)
        grad_first = lax.dot_general(x_rows, pre_grad, (((0,), (0,)), ((), ())), preferred_element_type=jnp.float32).astype(jnp.bfloat16)
        parts = jnp.einsum("rjf,djf->jrd", pre_grad.astype(jnp.float32).reshape(rows_per, N_DP, group), w_first.astype(jnp.float32).reshape(D, N_DP, group))
        parts = lax.optimization_barrier(parts.astype(jnp.bfloat16)).astype(jnp.float32)
        row_grads = jnp.sum(parts, axis=0).astype(jnp.bfloat16)
        gate_out = jnp.sum(hidden.astype(jnp.float32) * back, axis=1).astype(jnp.bfloat16)
        return grad_first, grad_second, row_grads, gate_out

    grad_in_weights, grad_out_weights, row_grads, gate_out = lax.map(expert_step, (disp_in, disp_cot, disp_gate, w_in, w_out))
    flat_rows = row_grads.reshape(EXPERTS * rows_per, D)
    token_grads = jnp.sum(flat_rows[index].astype(jnp.float32).reshape(TOKENS, 2, D), axis=1).astype(jnp.bfloat16)
    gate_grads = gate_out.reshape(-1)[index].reshape(TOKENS, 2)
    return token_grads, gate_grads, grad_in_weights, grad_out_weights
```

```python
import functools
import jax
import jax.numpy as jnp
from jax import lax
from jax.experimental import pallas as pl
from jax.experimental.pallas import tpu as pltpu
from jax.sharding import PartitionSpec as P

LANES = 128
GATHER_BYTES = 8 << 20


def flip(v, bit):
    return v + bit - 2 * bit * ((v // bit) % 2)


def fused_kernel(
    tok, feat, hid, zs, cap,
    pay_ref, w1_hbm, w2_hbm,
    grads_ref, gate_ref, xr_ref, sc_ref, hid_ref, pg_ref,
    G, W1, W2, CR, BE, TP, RC, S1, XA, SA, YA, YB, SB, XB, S3, ZR,
    wsem, zs_s, zs_r, xs_s, xs_r, ys_s, ys_r, dxs, dxr, dys, dyr, cs_s, cs_r,
    rc_s, rc_r, ra_s, ra_r, rb_s, rb_r, rz_s, rz_r,
):
    e = lax.axis_index("expert")
    z = lax.axis_index("dp")
    c, xb, yb = e % 2, (e // 2) % 2, (e // 4) % 2
    ec, ex, ey, exy = flip(e, 1), flip(e, 2), flip(e, 4), flip(flip(e, 2), 4)
    zp = [z]
    for d in range(1, zs):
        v = z
        for b in range(8):
            if (d >> b) & 1:
                v = flip(v, 1 << b)
        zp.append(v)
    wide = 2 * feat + LANES
    width = feat + LANES
    hw = (wide // LANES // 2) * LANES
    h0 = (width // LANES // 2) * LANES
    blk = lambda ee, zz: ee * zs + zz

    loads = [
        pltpu.make_async_copy(w1_hbm, W1, wsem.at[0]),
        pltpu.make_async_copy(w2_hbm, W2, wsem.at[1]),
    ]
    for l in loads:
        l.start()
    me = blk(e, z)
    G[pl.ds(me, 1)] = pay_ref[...][None]

    barrier = pltpu.get_barrier_semaphore()
    peers = [(ec, z), (ex, z), (ey, z)] + [(e, zp[d]) for d in range(1, zs)]
    for p in peers:
        pl.semaphore_signal(barrier, inc=1, device_id=p, device_id_type=pl.DeviceIdType.MESH)
    pl.semaphore_wait(barrier, len(peers))

    def rcopy(src, dst, ss, rs, dev):
        return pltpu.make_async_remote_copy(
            src_ref=src, dst_ref=dst, send_sem=ss, recv_sem=rs,
            device_id=dev, device_id_type=pl.DeviceIdType.MESH,
        )

    sends = []

    def go(cp):
        cp.start()
        sends.append(cp)
        return cp

    zc = [None]
    for d in range(1, zs):
        zc.append(go(rcopy(G.at[me], G.at[me], zs_s.at[d], zs_r.at[d], (e, zp[d]))))
    xc, yc, dx, dy, cc = [], [], [], [], []

    def core_send(b, k):
        cc.append(go(rcopy(G.at[b], G.at[b], cs_s.at[k], cs_r.at[k], (ec, z))))

    def diag(j):
        bx, by, bd = blk(ex, zp[j]), blk(ey, zp[j]), blk(exy, zp[j])
        xc[j].wait_recv()
        dy.append(go(rcopy(G.at[bx, :, pl.ds(0, hw)], G.at[bx, :, pl.ds(0, hw)],
                           dys.at[j], dyr.at[j], (ey, z))))
        core_send(bx, zs + j)
        yc[j].wait_recv()
        dx.append(go(rcopy(G.at[by, :, pl.ds(hw, wide - hw)], G.at[by, :, pl.ds(hw, wide - hw)],
                           dxs.at[j], dxr.at[j], (ex, z))))
        core_send(by, 2 * zs + j)

    for j in range(zs):
        b = blk(e, zp[j])
        if j:
            zc[j].wait_recv()
        xc.append(go(rcopy(G.at[b], G.at[b], xs_s.at[j], xs_r.at[j], (ex, z))))
        yc.append(go(rcopy(G.at[b], G.at[b], ys_s.at[j], ys_r.at[j], (ey, z))))
        core_send(b, j)
        if j:
            diag(j - 1)
    diag(zs - 1)
    for j in range(zs):
        dy[j].wait_recv()
        dx[j].wait_recv()
        core_send(blk(exy, zp[j]), 3 * zs + j)
    for k in cc:
        k.wait_recv()

    blocks = G.shape[0]
    per = blocks // 2
    gt, gr = per * tok, per * cap
    ef = e.astype(jnp.float32)
    picks, metas = [], []
    ti = lax.broadcasted_iota(jnp.int32, (gt, gt), 0)
    tj = lax.broadcasted_iota(jnp.int32, (gt, gt), 1)
    lower = jnp.where((ti // tok == tj // tok) & (tj < ti), 1.0, 0.0).astype(jnp.bfloat16)
    base = ((lax.broadcasted_iota(jnp.int32, (gt, gr), 0) // tok) * cap).astype(jnp.float32)
    lane = lax.broadcasted_iota(jnp.int32, (gt, gr), 1).astype(jnp.float32)
    tdims = (((0,), (0,)), ((), ()))
    for g in range(2):
        m = G[g * per:(g + 1) * per, :, 2 * feat:].reshape(gt, LANES).astype(jnp.float32)
        m0 = m[:, 0:1] == ef
        m1 = m[:, 1:2] == ef
        mask = jnp.where(m0 | m1, 1.0, 0.0)
        gtok = jnp.where(m0, m[:, 2:3], 0.0) + jnp.where(m1, m[:, 3:4], 0.0)
        slot = jnp.dot(lower, jnp.broadcast_to(mask, (gt, gr)).astype(jnp.bfloat16),
                       preferred_element_type=jnp.float32)
        pick = jnp.where((slot + base == lane) & (mask > 0.0), 1.0, 0.0).astype(jnp.bfloat16)
        picks.append(pick)
        metas.append(m)
        gate = lax.dot_general(pick, jnp.broadcast_to(gtok, (gt, LANES)).astype(jnp.bfloat16),
                               tdims, preferred_element_type=jnp.float32)
        BE[g * gr:(g + 1) * gr, :] = gate
        xg = G[g * per:(g + 1) * per, :, 0:feat].reshape(gt, feat)
        xr_ref[g * gr:(g + 1) * gr, :] = lax.dot_general(
            pick, xg, tdims, preferred_element_type=jnp.float32).astype(jnp.bfloat16)
        cg = G[g * per:(g + 1) * per, :, feat:2 * feat].reshape(gt, feat)
        cr = lax.dot_general(pick, cg, tdims, preferred_element_type=jnp.float32)
        CR[g * gr:(g + 1) * gr, :] = cr.astype(jnp.bfloat16)
        sc_ref[g * gr:(g + 1) * gr, :] = (gate[:, 0:1] * cr).astype(jnp.bfloat16)

    for l in loads:
        l.wait()
    rows = 2 * gr
    step = min(hid, 256)

    def hidden_step(i, acc):
        f = pl.multiple_of(i * step, step)
        pre = jnp.dot(xr_ref[...], W1[:, pl.ds(f, step)], preferred_element_type=jnp.float32)
        back = lax.dot_general(CR[...], W2[pl.ds(f, step), :], (((1,), (1,)), ((), ())),
                               preferred_element_type=jnp.float32)
        cdf = 0.5 * (1.0 + lax.erf(pre * 0.7071067811865476))
        pdf = 0.3989422804014327 * jnp.exp(-0.5 * pre * pre)
        h = (pre * cdf).astype(jnp.bfloat16)
        hid_ref[:, pl.ds(f, step)] = h
        pg_ref[:, pl.ds(f, step)] = (BE[:, 0:1] * back * (cdf + pre * pdf)).astype(jnp.bfloat16)
        return acc + jnp.sum(h.astype(jnp.float32) * back, axis=1, keepdims=True)

    gsum = lax.fori_loop(0, hid // step, hidden_step, jnp.zeros((rows, 1), jnp.float32))
    hi = gsum.astype(jnp.bfloat16).astype(jnp.float32)
    li = lax.broadcasted_iota(jnp.int32, (rows, LANES), 1)
    extra = jnp.where(li < 2, hi, gsum - hi).astype(jnp.bfloat16)

    def place(lo, hi_):
        n = min(hi_, feat) - lo
        part = lax.dot_general(pg_ref[...], W1[lo:lo + n, :], (((1,), (1,)), ((), ())),
                               preferred_element_type=jnp.float32).astype(jnp.bfloat16)
        for g in range(2):
            t = jnp.dot(picks[g], part[g * gr:(g + 1) * gr], preferred_element_type=jnp.float32)
            TP[2 * g:2 * g + 2, :, :, :, lo:lo + n] = t.astype(jnp.bfloat16).reshape(2, 2, zs, tok, n)
            if hi_ > feat:
                v = jnp.dot(picks[g], extra[g * gr:(g + 1) * gr], preferred_element_type=jnp.float32)
                tl = lax.broadcasted_iota(jnp.int32, (gt, LANES), 1)
                m = metas[g]
                own = jnp.where(tl % 2 == 0, m[:, 0:1], m[:, 1:2]) == ef
                v = jnp.where(own & (tl < 4), v, 0.0)
                TP[2 * g:2 * g + 2, :, :, :, feat:] = v.astype(jnp.bfloat16).reshape(2, 2, zs, tok, LANES)

    def core_swap(i, lo, n):
        return go(rcopy(TP.at[:, 1 - c, :, :, pl.ds(lo, n)], RC.at[:, :, :, pl.ds(lo, n)],
                        rc_s.at[i], rc_r.at[i], (ec, z)))

    def core_add(lo, n):
        s = (TP[:, pl.ds(c, 1), :, :, lo:lo + n].reshape(4, zs, tok, n).astype(jnp.float32)
             + RC[:, :, :, lo:lo + n].astype(jnp.float32))
        S1[:, :, :, :, lo:lo + n] = s.astype(jnp.bfloat16).reshape(2, 2, zs, tok, n)

    n1 = width - h0
    f32 = jnp.float32
    place(0, h0)
    s0 = core_swap(0, 0, h0)
    place(h0, width)
    s1 = core_swap(1, h0, n1)
    s0.wait_recv()
    core_add(0, h0)
    a0 = go(rcopy(S1.at[:, 1 - xb, :, :, pl.ds(0, h0)], XA, ra_s.at[0], ra_r.at[0], (ex, z)))
    s1.wait_recv()
    core_add(h0, n1)
    a1 = go(rcopy(S1.at[1 - yb, :, :, :, pl.ds(h0, n1)], YB, ra_s.at[1], ra_r.at[1], (ey, z)))
    a0.wait_recv()
    SA[...] = (S1[:, pl.ds(xb, 1), :, :, 0:h0].reshape(2, zs, tok, h0).astype(f32)
               + XA[...].astype(f32)).astype(jnp.bfloat16)
    b0 = go(rcopy(SA.at[1 - yb], YA, rb_s.at[0], rb_r.at[0], (ey, z)))
    a1.wait_recv()
    SB[...] = (S1[pl.ds(yb, 1), :, :, :, h0:].reshape(2, zs, tok, n1).astype(f32)
               + YB[...].astype(f32)).astype(jnp.bfloat16)
    b1 = go(rcopy(SB.at[1 - xb], XB, rb_s.at[1], rb_r.at[1], (ex, z)))
    b0.wait_recv()
    S3[:, :, 0:h0] = (SA[pl.ds(yb, 1)].reshape(zs, tok, h0).astype(f32)
                      + YA[...].astype(f32)).astype(jnp.bfloat16)
    b1.wait_recv()
    S3[:, :, h0:] = (SB[pl.ds(xb, 1)].reshape(zs, tok, n1).astype(f32)
                     + XB[...].astype(f32)).astype(jnp.bfloat16)
    zcs = [go(rcopy(S3.at[zp[d]], ZR.at[d - 1], rz_s.at[d], rz_r.at[d], (e, zp[d])))
           for d in range(1, zs)]
    total = S3[pl.ds(z, 1)].reshape(tok, width).astype(f32)
    for d in range(1, zs):
        zcs[d - 1].wait_recv()
        total = total + ZR[d - 1].astype(f32)
    grads_ref[...] = total[:, 0:feat].astype(jnp.bfloat16)
    gate_ref[...] = total[:, feat:]
    for s in sends:
        s.wait_send()


def fused(tokens, cotangent, expert_ids, gates, w_in, w_out):
    tok, feat = tokens.shape
    experts, zs = lax.axis_size("expert"), lax.axis_size("dp")
    hid = w_in.shape[2]
    cap = max(2, 4 * tok // experts)
    bf = jnp.bfloat16
    meta = jnp.concatenate(
        [expert_ids.astype(bf), gates, jnp.zeros((tok, LANES - 4), bf)], axis=1)
    pay = jnp.concatenate([tokens, cotangent, meta], axis=1)
    blocks = experts * zs
    rows = blocks * cap
    width = feat + LANES
    h0 = (width // LANES // 2) * LANES
    n1 = width - h0
    vm = pl.BlockSpec(memory_space=pltpu.VMEM)
    hbm = pl.BlockSpec(memory_space=pl.ANY)
    dma = lambda n: pltpu.SemaphoreType.DMA((n,))
    V = lambda *s: pltpu.VMEM(s, bf)
    sd = jax.ShapeDtypeStruct
    grads, gate, xr, sc, hd, pg = pl.pallas_call(
        functools.partial(fused_kernel, tok, feat, hid, zs, cap),
        out_shape=(
            sd((tok, feat), bf), sd((tok, LANES), jnp.float32), sd((rows, feat), bf),
            sd((rows, feat), bf), sd((rows, hid), bf), sd((rows, hid), bf),
        ),
        in_specs=[vm, hbm, hbm],
        out_specs=(vm,) * 6,
        scratch_shapes=[
            V(blocks, tok, 2 * feat + LANES), V(feat, hid), V(hid, feat), V(rows, feat),
            pltpu.VMEM((rows, LANES), jnp.float32),
            V(4, 2, zs, tok, width), V(4, zs, tok, width), V(2, 2, zs, tok, width),
            V(2, zs, tok, h0), V(2, zs, tok, h0), V(zs, tok, h0),
            V(2, zs, tok, n1), V(2, zs, tok, n1), V(zs, tok, n1),
            V(zs, tok, width), V(zs - 1, tok, width),
            dma(2), dma(zs), dma(zs), dma(zs), dma(zs), dma(zs), dma(zs),
            dma(zs), dma(zs), dma(zs), dma(zs), dma(4 * zs), dma(4 * zs),
            dma(2), dma(2), dma(2), dma(2), dma(2), dma(2), dma(zs), dma(zs),
        ],
        compiler_params=pltpu.CompilerParams(
            collective_id=0, has_side_effects=True, vmem_limit_bytes=48 << 20),
        cost_estimate=pl.CostEstimate(
            flops=6 * rows * feat * hid, bytes_accessed=4 * feat * hid, transcendentals=0),
    )(pay, w_in[0], w_out[0])
    dims = (((0,), (0,)), ((), ()))
    g1 = lax.dot_general(xr, pg, dims, preferred_element_type=jnp.float32).astype(bf)
    g2 = lax.dot_general(hd, sc, dims, preferred_element_type=jnp.float32).astype(bf)
    gate_grads = (gate[:, 0:2] + gate[:, 2:4]).astype(bf)
    return grads, gate_grads, g1[None], g2[None]


def normal_parts(pre):
    cdf = 0.5 * (1.0 + lax.erf(pre * 0.7071067811865476))
    pdf = 0.3989422804014327 * jnp.exp(-0.5 * pre * pre)
    return (cdf, pdf)


def per_device(tokens, cotangent, expert_ids, gates, w_in, w_out):
    tok = tokens.shape[0]
    feat = tokens.shape[1]
    experts = lax.axis_size("expert")
    cap = max(2, 4 * tok // experts)
    assign = 2 * tok
    ids = expert_ids.reshape(assign)
    onehot = (ids[:, None] == jnp.arange(experts, dtype=jnp.int32)[None, :]).astype(jnp.float32)
    lower = (jnp.arange(assign)[:, None] > jnp.arange(assign)[None, :]).astype(jnp.float32)
    before = jnp.dot(lower, onehot, preferred_element_type=jnp.float32)
    slot = jnp.sum(before * onehot, axis=1).astype(jnp.int32)
    target = ids * cap + slot
    pick = (jnp.arange(experts * cap, dtype=jnp.int32)[:, None] == target[None, :]).astype(
        jnp.bfloat16
    )
    src_in = jnp.repeat(tokens, 2, axis=0)
    src_cot = jnp.repeat(cotangent, 2, axis=0)
    send_in = (
        jnp.dot(pick, src_in, preferred_element_type=jnp.float32)
        .astype(jnp.bfloat16)
        .reshape(experts, cap, feat)
    )
    send_cot = (
        jnp.dot(pick, src_cot, preferred_element_type=jnp.float32)
        .astype(jnp.bfloat16)
        .reshape(experts, cap, feat)
    )
    send_gate = (
        jnp.dot(pick, gates.reshape(assign, 1), preferred_element_type=jnp.float32)
        .astype(jnp.bfloat16)
        .reshape(experts, cap)
    )
    w_first = w_in[0]
    w_second = w_out[0]
    arrived = (
        lax.all_to_all(send_in, "expert", split_axis=0, concat_axis=0, tiled=True),
        lax.all_to_all(send_cot, "expert", split_axis=0, concat_axis=0, tiled=True),
        lax.all_to_all(send_gate, "expert", split_axis=0, concat_axis=0, tiled=True),
    )
    x_blocks = lax.all_gather(arrived[0], "dp", axis=0, tiled=True)
    cot_blocks = lax.all_gather(arrived[1], "dp", axis=0, tiled=True)
    gate_blocks = lax.all_gather(arrived[2], "dp", axis=0, tiled=True)
    count = x_blocks.shape[0] * x_blocks.shape[1]
    x_rows = x_blocks.reshape(count, feat)
    cot_rows = cot_blocks.reshape(count, feat)
    gate_f = gate_blocks.reshape(count, 1).astype(jnp.float32)
    pre = jnp.dot(x_rows, w_first, preferred_element_type=jnp.float32)
    cdf, pdf = normal_parts(pre)
    hidden = (pre * cdf).astype(jnp.bfloat16)
    back = lax.dot_general(
        cot_rows, w_second, (((1,), (1,)), ((), ())), preferred_element_type=jnp.float32
    )
    scaled = (gate_f * cot_rows.astype(jnp.float32)).astype(jnp.bfloat16)
    grad_second = lax.dot_general(
        hidden, scaled, (((0,), (0,)), ((), ())), preferred_element_type=jnp.float32
    )
    pre_grad = (gate_f * back * (cdf + pre * pdf)).astype(jnp.bfloat16)
    grad_first = lax.dot_general(
        x_rows, pre_grad, (((0,), (0,)), ((), ())), preferred_element_type=jnp.float32
    )
    row_part = lax.dot_general(
        pre_grad, w_first, (((1,), (1,)), ((), ())), preferred_element_type=jnp.float32
    ).astype(jnp.bfloat16)
    gate_part = jnp.sum(hidden.astype(jnp.float32) * back, axis=1)
    row_sums = lax.psum_scatter(row_part, "dp", scatter_dimension=0, tiled=True)
    gate_sums = lax.psum_scatter(gate_part, "dp", scatter_dimension=0, tiled=True)
    row_back = row_sums.reshape(experts, cap, feat)
    gate_back = gate_sums.astype(jnp.bfloat16).reshape(experts, cap)
    back_rows, back_gate = (
        lax.all_to_all(row_back, "expert", split_axis=0, concat_axis=0, tiled=True),
        lax.all_to_all(gate_back, "expert", split_axis=0, concat_axis=0, tiled=True),
    )
    flat_back = back_rows.reshape(experts * cap, feat)
    per_assign = lax.dot_general(
        pick, flat_back, (((0,), (0,)), ((), ())), preferred_element_type=jnp.float32
    )
    token_grads = jnp.sum(per_assign.reshape(tok, 2, feat), axis=1).astype(jnp.bfloat16)
    gate_assign = lax.dot_general(
        pick,
        back_gate.reshape(experts * cap, 1),
        (((0,), (0,)), ((), ())),
        preferred_element_type=jnp.float32,
    )
    gate_grads = gate_assign.reshape(tok, 2).astype(jnp.bfloat16)
    grad_in_weights = grad_first.astype(jnp.bfloat16)[None]
    grad_out_weights = grad_second.astype(jnp.bfloat16)[None]
    return (token_grads, gate_grads, grad_in_weights, grad_out_weights)


def solution(mesh):
    in_specs = (
        P(("expert", "dp"), None),
        P(("expert", "dp"), None),
        P(("expert", "dp"), None),
        P(("expert", "dp"), None),
        P("expert", None, "dp"),
        P("expert", "dp", None),
    )
    out_specs = (
        P(("expert", "dp"), None),
        P(("expert", "dp"), None),
        P("expert", None, "dp"),
        P("expert", "dp", None),
    )
    sizes = dict(mesh.shape)

    def run(tokens, *rest):
        zs = sizes["dp"]
        row_bytes = 2 * (2 * tokens.shape[1] + LANES)
        small = tokens.shape[0] * row_bytes <= GATHER_BYTES
        cube = sizes["expert"] == 8 and zs > 1 and zs & (zs - 1) == 0
        plan = fused if small and cube else per_device
        return mapped(plan)(tokens, *rest)

    def mapped(plan):
        return jax.shard_map(
            plan, mesh=mesh, in_specs=in_specs, out_specs=out_specs, check_vma=False
        )

    return run
```

```python
import functools
import jax
import jax.numpy as jnp
from jax import lax
from jax.experimental import pallas as pl
from jax.experimental.pallas import tpu as pltpu
from jax.sharding import PartitionSpec as P

LANES = 128
GATHER_BYTES = 8 << 20


def flip(v, bit):
    return v + bit - 2 * bit * ((v // bit) % 2)


def fused_kernel(
    tok, feat, hid, zs, cap, chunks,
    tok_ref, cot_ref, ids_ref, gates_ref, w1_hbm, w2_hbm,
    grads_ref, gate_ref, xr_ref, sc_ref, hid_ref, pg_ref,
    G, W1, W2, CR, BE, TP, RC, S1, A1, A2, A3, S3, ZR,
    wsem, zs_s, zs_r, xs_s, xs_r, ys_s, ys_r, dxs, dxr, dys, dyr, cs_s, cs_r,
    rc_s, rc_r, ra_s, ra_r, rb_s, rb_r, rz_s, rz_r,
):
    f32, bf = jnp.float32, jnp.bfloat16
    e = lax.axis_index("expert")
    z = lax.axis_index("dp")
    experts = G.shape[0] // zs
    c, xb, yb = e % 2, (e // 2) % 2, (e // 4) % 2
    ec, ex, ey, exy = flip(e, 1), flip(e, 2), flip(e, 4), flip(flip(e, 2), 4)
    zp = [z]
    for d in range(1, zs):
        v = z
        for b in range(8):
            if (d >> b) & 1:
                v = flip(v, 1 << b)
        zp.append(v)
    wide = 2 * feat + LANES
    hw = (wide // LANES // 2) * LANES
    blk = lambda ee, j: j * experts + ee

    loads = [
        pltpu.make_async_copy(w1_hbm, W1, wsem.at[0]),
        pltpu.make_async_copy(w2_hbm, W2, wsem.at[1]),
    ]
    for l in loads:
        l.start()
    eye = lax.broadcasted_iota(jnp.int32, (tok, tok), 0) == lax.broadcasted_iota(
        jnp.int32, (tok, tok), 1)
    col = lambda r: jnp.sum(jnp.where(eye, r, 0.0), axis=1, keepdims=True)
    ids_f, gates_f = ids_ref[...].astype(f32), gates_ref[...].astype(f32)
    ln = lax.broadcasted_iota(jnp.int32, (tok, LANES), 1)
    meta = jnp.zeros((tok, LANES), f32)
    for k, r in enumerate((ids_f[0:1], ids_f[1:2], gates_f[0:1], gates_f[1:2])):
        meta = jnp.where(ln == k, col(r), meta)
    G[pl.ds(e, 1), :, 0:feat] = tok_ref[...][None]
    G[pl.ds(e, 1), :, feat:2 * feat] = cot_ref[...][None]
    G[pl.ds(e, 1), :, 2 * feat:] = meta.astype(bf)[None]

    barrier = pltpu.get_barrier_semaphore()
    peers = [(ec, z), (ex, z), (ey, z)] + [(e, zp[d]) for d in range(1, zs)]
    for p in peers:
        pl.semaphore_signal(barrier, inc=1, device_id=p, device_id_type=pl.DeviceIdType.MESH)
    pl.semaphore_wait(barrier, len(peers))

    sends = []

    def go(src, dst, ss, rs, dev):
        cp = pltpu.make_async_remote_copy(
            src_ref=src, dst_ref=dst, send_sem=ss, recv_sem=rs,
            device_id=dev, device_id_type=pl.DeviceIdType.MESH,
        )
        cp.start()
        sends.append(cp)
        return cp

    xc, yc, dx, dy, cc = [], [], [], [], {}
    zc = [None]

    def core_send(b, j, k):
        cc[j, k] = go(G.at[b], G.at[b], cs_s.at[k * zs + j], cs_r.at[k * zs + j], (ec, z))

    def plane(j):
        b = blk(e, j)
        xc.append(go(G.at[b], G.at[b], xs_s.at[j], xs_r.at[j], (ex, z)))
        yc.append(go(G.at[b], G.at[b], ys_s.at[j], ys_r.at[j], (ey, z)))
        core_send(b, j, 0)

    def diag(j):
        bx, by = blk(ex, j), blk(ey, j)
        xc[j].wait_recv()
        v = G.at[bx, :, pl.ds(0, hw)]
        dy.append(go(v, v, dys.at[j], dyr.at[j], (ey, z)))
        core_send(bx, j, 1)
        yc[j].wait_recv()
        v = G.at[by, :, pl.ds(hw, wide - hw)]
        dx.append(go(v, v, dxs.at[j], dxr.at[j], (ex, z)))
        core_send(by, j, 2)

    def finish(j):
        dy[j].wait_recv()
        dx[j].wait_recv()
        core_send(blk(exy, j), j, 3)

    per = G.shape[0] // 2
    zh = zs // 2
    gt, gr = per * tok, per * cap
    ef = e.astype(f32)
    ti = lax.broadcasted_iota(jnp.int32, (gt, gt), 0)
    tj = lax.broadcasted_iota(jnp.int32, (gt, gt), 1)
    lower = jnp.where((ti // tok == tj // tok) & (tj < ti), 1.0, 0.0).astype(bf)
    base = ((lax.broadcasted_iota(jnp.int32, (gt, gr), 0) // tok) * cap).astype(f32)
    lane = lax.broadcasted_iota(jnp.int32, (gt, gr), 1).astype(f32)
    tdims = (((0,), (0,)), ((), ()))
    ndims = (((1,), (1,)), ((), ()))
    picks, metas, gsums = [], [], [None, None]
    step = min(hid, 256)

    def pick_group(g):
        for j in range(g * zh, (g + 1) * zh):
            for k in range(4):
                cc[j, k].wait_recv()
        m = G[g * per:(g + 1) * per, :, 2 * feat:].reshape(gt, LANES).astype(f32)
        m0 = m[:, 0:1] == ef
        m1 = m[:, 1:2] == ef
        mask = jnp.where(m0 | m1, 1.0, 0.0)
        gtok = jnp.where(m0, m[:, 2:3], 0.0) + jnp.where(m1, m[:, 3:4], 0.0)
        slot = jnp.dot(lower, jnp.broadcast_to(mask, (gt, gr)).astype(bf),
                       preferred_element_type=f32)
        pick = jnp.where((slot + base == lane) & (mask > 0.0), 1.0, 0.0).astype(bf)
        picks.append(pick)
        metas.append(m)
        gate = lax.dot_general(pick, jnp.broadcast_to(gtok, (gt, LANES)).astype(bf),
                               tdims, preferred_element_type=f32)
        sl = slice(g * gr, (g + 1) * gr)
        BE[sl, :] = gate
        xg = G[g * per:(g + 1) * per, :, 0:feat].reshape(gt, feat)
        xr_ref[sl, :] = lax.dot_general(pick, xg, tdims, preferred_element_type=f32).astype(bf)
        cg = G[g * per:(g + 1) * per, :, feat:2 * feat].reshape(gt, feat)
        cr = lax.dot_general(pick, cg, tdims, preferred_element_type=f32)
        CR[sl, :] = cr.astype(bf)
        sc_ref[sl, :] = (gate[:, 0:1] * cr).astype(bf)

    def hidden_step(g, i):
        sl, fs = slice(g * gr, (g + 1) * gr), slice(i * step, (i + 1) * step)
        pre = jnp.dot(xr_ref[sl, :], W1[:, fs], preferred_element_type=f32)
        back = lax.dot_general(CR[sl, :], W2[fs, :], ndims, preferred_element_type=f32)
        cdf = 0.5 * (1.0 + lax.erf(pre * 0.7071067811865476))
        pdf = 0.3989422804014327 * jnp.exp(-0.5 * pre * pre)
        h = (pre * cdf).astype(bf)
        hid_ref[sl, fs] = h
        pg_ref[sl, fs] = (BE[sl, 0:1] * back * (cdf + pre * pdf)).astype(bf)
        t = jnp.sum(h.astype(f32) * back, axis=1, keepdims=True)
        gsums[g] = t if gsums[g] is None else gsums[g] + t

    for d in range(1, zs):
        zc.append(go(G.at[blk(e, 0)], G.at[blk(e, d)], zs_s.at[d], zs_r.at[d], (e, zp[d])))
    for j in range(zs):
        if j:
            zc[j].wait_recv()
        plane(j)
        if j:
            diag(j - 1)
    for j in range(zh):
        finish(j)
    steps = hid // step
    pick_group(0)
    for l in loads:
        l.wait()
    for i in range(steps // 2):
        hidden_step(0, i)
    diag(zs - 1)
    for j in range(zh, zs - 1):
        finish(j)
    for i in range(steps // 2, steps):
        hidden_step(0, i)
    finish(zs - 1)
    pick_group(1)
    for i in range(steps):
        hidden_step(1, i)

    def place(i):
        lo, w = chunks[i]
        n = min(lo + w, feat) - lo
        part = lax.dot_general(pg_ref[...], W1[lo:lo + n, :], ndims,
                               preferred_element_type=f32).astype(bf)
        for g in range(2):
            js, rs = slice(g * zh, (g + 1) * zh), slice(g * gr, (g + 1) * gr)
            t = jnp.dot(picks[g], part[rs], preferred_element_type=f32)
            TP[js, :, :, :, :, lo:lo + n] = t.astype(bf).reshape(zh, 2, 2, 2, tok, n)
            if lo + w > feat:
                hi = gsums[g].astype(bf).astype(f32)
                li = lax.broadcasted_iota(jnp.int32, (gr, LANES), 1)
                extra = jnp.where(li < 2, hi, gsums[g] - hi).astype(bf)
                v = jnp.dot(picks[g], extra, preferred_element_type=f32)
                tl = lax.broadcasted_iota(jnp.int32, (gt, LANES), 1)
                m = metas[g]
                own = jnp.where(tl % 2 == 0, m[:, 0:1], m[:, 1:2]) == ef
                v = jnp.where(own & (tl < 4), v, 0.0)
                TP[js, :, :, :, :, feat:] = v.astype(bf).reshape(zh, 2, 2, 2, tok, LANES)
        ds = pl.ds(lo, w)
        swaps.append(go(TP.at[:, :, :, 1 - c, :, ds], RC.at[:, :, :, :, ds],
                        rc_s.at[i], rc_r.at[i], (ec, z)))

    swaps, firsts, seconds, lasts = [], [], [], []

    def after_core(i):
        lo, w = chunks[i]
        ds = pl.ds(lo, w)
        swaps[i].wait_recv()
        s = (TP[:, :, :, pl.ds(c, 1), :, lo:lo + w].reshape(zs, 2, 2, tok, w).astype(f32)
             + RC[:, :, :, :, lo:lo + w].astype(f32))
        S1[:, :, :, :, lo:lo + w] = s.astype(bf)
        if i % 2 == 0:
            src, dev = S1.at[:, :, 1 - xb, :, ds], (ex, z)
        else:
            src, dev = S1.at[:, 1 - yb, :, :, ds], (ey, z)
        firsts.append(go(src, A1.at[:, :, :, ds], ra_s.at[i], ra_r.at[i], dev))

    def after_first(i):
        lo, w = chunks[i]
        ds = pl.ds(lo, w)
        firsts[i].wait_recv()
        if i % 2 == 0:
            mine, other, dev = S1[:, :, pl.ds(xb, 1), :, lo:lo + w], 1 - yb, (ey, z)
        else:
            mine, other, dev = S1[:, pl.ds(yb, 1), :, :, lo:lo + w], 1 - xb, (ex, z)
        A2[:, :, :, lo:lo + w] = (mine.reshape(zs, 2, tok, w).astype(f32)
                                  + A1[:, :, :, lo:lo + w].astype(f32)).astype(bf)
        seconds.append(go(A2.at[:, other, :, ds], A3.at[:, :, ds],
                          rb_s.at[i], rb_r.at[i], dev))

    def after_second(i):
        lo, w = chunks[i]
        ds = pl.ds(lo, w)
        seconds[i].wait_recv()
        own = yb if i % 2 == 0 else xb
        S3[:, :, lo:lo + w] = (A2[:, pl.ds(own, 1), :, lo:lo + w].reshape(zs, tok, w).astype(f32)
                               + A3[:, :, lo:lo + w].astype(f32)).astype(bf)
        lasts.append([go(S3.at[d, :, ds], ZR.at[d - 1, :, ds],
                         rz_s.at[i * zs + d], rz_r.at[i * zs + d], (e, zp[d]))
                      for d in range(1, zs)])

    n = len(chunks)
    for t in range(n + 5):
        for lag, stage in ((0, place), (1, after_core), (3, after_first), (5, after_second)):
            if 0 <= t - lag < n:
                stage(t - lag)
    for i, (lo, w) in enumerate(chunks):
        total = S3[0, :, lo:lo + w].astype(f32)
        for d in range(1, zs):
            lasts[i][d - 1].wait_recv()
            total = total + ZR[d - 1, :, lo:lo + w].astype(f32)
        m = min(lo + w, feat) - lo
        grads_ref[:, lo:lo + m] = total[:, 0:m].astype(bf)
        if m < w:
            row = lambda k: jnp.sum(
                jnp.where(eye, total[:, m + k:m + k + 1] + total[:, m + k + 2:m + k + 3], 0.0),
                axis=0, keepdims=True)
            first = lax.broadcasted_iota(jnp.int32, (2, tok), 0) == 0
            gate_ref[...] = jnp.where(first, row(0), row(1)).astype(bf)
    for s in sends:
        s.wait_send()


def fused(tokens, cotangent, expert_ids, gates, w_in, w_out):
    tok, feat = tokens.shape
    experts, zs = lax.axis_size("expert"), lax.axis_size("dp")
    hid = w_in.shape[2]
    cap = max(2, 4 * tok // experts)
    bf = jnp.bfloat16
    blocks = experts * zs
    rows = blocks * cap
    width = feat + LANES
    tiles = width // LANES
    a, b = tiles // 4, tiles // 2 - tiles // 4
    widths = (a, b, b, tiles - a - 2 * b)
    chunks, at = [], 0
    for w in widths:
        chunks.append((at * LANES, w * LANES))
        at += w
    nc = len(chunks)
    vm = pl.BlockSpec(memory_space=pltpu.VMEM)
    hbm = pl.BlockSpec(memory_space=pl.ANY)
    dma = lambda n: pltpu.SemaphoreType.DMA((n,))
    V = lambda *s: pltpu.VMEM(s, bf)
    sd = jax.ShapeDtypeStruct
    grads, gate, xr, sc, hd, pg = pl.pallas_call(
        functools.partial(fused_kernel, tok, feat, hid, zs, cap, tuple(chunks)),
        out_shape=(
            sd((tok, feat), bf), sd((2, tok), bf), sd((rows, feat), bf),
            sd((rows, feat), bf), sd((rows, hid), bf), sd((rows, hid), bf),
        ),
        in_specs=[vm, vm, vm, vm, hbm, hbm],
        out_specs=(vm,) * 6,
        scratch_shapes=[
            V(blocks, tok, 2 * feat + LANES), V(feat, hid), V(hid, feat), V(rows, feat),
            pltpu.VMEM((rows, LANES), jnp.float32),
            V(zs, 2, 2, 2, tok, width), V(zs, 2, 2, tok, width), V(zs, 2, 2, tok, width),
            V(zs, 2, tok, width), V(zs, 2, tok, width), V(zs, tok, width),
            V(zs, tok, width), V(zs - 1, tok, width),
            dma(2), dma(zs), dma(zs), dma(zs), dma(zs), dma(zs), dma(zs),
            dma(zs), dma(zs), dma(zs), dma(zs), dma(4 * zs), dma(4 * zs),
            dma(nc), dma(nc), dma(nc), dma(nc), dma(nc), dma(nc), dma(nc * zs), dma(nc * zs),
        ],
        compiler_params=pltpu.CompilerParams(
            collective_id=0, has_side_effects=True, vmem_limit_bytes=48 << 20),
        cost_estimate=pl.CostEstimate(
            flops=6 * rows * feat * hid, bytes_accessed=4 * feat * hid, transcendentals=0),
    )(tokens, cotangent, expert_ids.T, gates.T, w_in[0], w_out[0])
    dims = (((0,), (0,)), ((), ()))
    g1 = lax.dot_general(xr, pg, dims, preferred_element_type=jnp.float32).astype(bf)
    g2 = lax.dot_general(hd, sc, dims, preferred_element_type=jnp.float32).astype(bf)
    return grads, gate.T, g1[None], g2[None]


def normal_parts(pre):
    cdf = 0.5 * (1.0 + lax.erf(pre * 0.7071067811865476))
    pdf = 0.3989422804014327 * jnp.exp(-0.5 * pre * pre)
    return (cdf, pdf)


def per_device(tokens, cotangent, expert_ids, gates, w_in, w_out):
    tok = tokens.shape[0]
    feat = tokens.shape[1]
    experts = lax.axis_size("expert")
    cap = max(2, 4 * tok // experts)
    assign = 2 * tok
    ids = expert_ids.reshape(assign)
    onehot = (ids[:, None] == jnp.arange(experts, dtype=jnp.int32)[None, :]).astype(jnp.float32)
    lower = (jnp.arange(assign)[:, None] > jnp.arange(assign)[None, :]).astype(jnp.float32)
    before = jnp.dot(lower, onehot, preferred_element_type=jnp.float32)
    slot = jnp.sum(before * onehot, axis=1).astype(jnp.int32)
    target = ids * cap + slot
    pick = (jnp.arange(experts * cap, dtype=jnp.int32)[:, None] == target[None, :]).astype(
        jnp.bfloat16
    )
    src_in = jnp.repeat(tokens, 2, axis=0)
    src_cot = jnp.repeat(cotangent, 2, axis=0)
    send_in = (
        jnp.dot(pick, src_in, preferred_element_type=jnp.float32)
        .astype(jnp.bfloat16)
        .reshape(experts, cap, feat)
    )
    send_cot = (
        jnp.dot(pick, src_cot, preferred_element_type=jnp.float32)
        .astype(jnp.bfloat16)
        .reshape(experts, cap, feat)
    )
    send_gate = (
        jnp.dot(pick, gates.reshape(assign, 1), preferred_element_type=jnp.float32)
        .astype(jnp.bfloat16)
        .reshape(experts, cap)
    )
    w_first = w_in[0]
    w_second = w_out[0]
    arrived = (
        lax.all_to_all(send_in, "expert", split_axis=0, concat_axis=0, tiled=True),
        lax.all_to_all(send_cot, "expert", split_axis=0, concat_axis=0, tiled=True),
        lax.all_to_all(send_gate, "expert", split_axis=0, concat_axis=0, tiled=True),
    )
    x_blocks = lax.all_gather(arrived[0], "dp", axis=0, tiled=True)
    cot_blocks = lax.all_gather(arrived[1], "dp", axis=0, tiled=True)
    gate_blocks = lax.all_gather(arrived[2], "dp", axis=0, tiled=True)
    count = x_blocks.shape[0] * x_blocks.shape[1]
    x_rows = x_blocks.reshape(count, feat)
    cot_rows = cot_blocks.reshape(count, feat)
    gate_f = gate_blocks.reshape(count, 1).astype(jnp.float32)
    pre = jnp.dot(x_rows, w_first, preferred_element_type=jnp.float32)
    cdf, pdf = normal_parts(pre)
    hidden = (pre * cdf).astype(jnp.bfloat16)
    back = lax.dot_general(
        cot_rows, w_second, (((1,), (1,)), ((), ())), preferred_element_type=jnp.float32
    )
    scaled = (gate_f * cot_rows.astype(jnp.float32)).astype(jnp.bfloat16)
    grad_second = lax.dot_general(
        hidden, scaled, (((0,), (0,)), ((), ())), preferred_element_type=jnp.float32
    )
    pre_grad = (gate_f * back * (cdf + pre * pdf)).astype(jnp.bfloat16)
    grad_first = lax.dot_general(
        x_rows, pre_grad, (((0,), (0,)), ((), ())), preferred_element_type=jnp.float32
    )
    row_part = lax.dot_general(
        pre_grad, w_first, (((1,), (1,)), ((), ())), preferred_element_type=jnp.float32
    ).astype(jnp.bfloat16)
    gate_part = jnp.sum(hidden.astype(jnp.float32) * back, axis=1)
    row_sums = lax.psum_scatter(row_part, "dp", scatter_dimension=0, tiled=True)
    gate_sums = lax.psum_scatter(gate_part, "dp", scatter_dimension=0, tiled=True)
    row_back = row_sums.reshape(experts, cap, feat)
    gate_back = gate_sums.astype(jnp.bfloat16).reshape(experts, cap)
    back_rows, back_gate = (
        lax.all_to_all(row_back, "expert", split_axis=0, concat_axis=0, tiled=True),
        lax.all_to_all(gate_back, "expert", split_axis=0, concat_axis=0, tiled=True),
    )
    flat_back = back_rows.reshape(experts * cap, feat)
    per_assign = lax.dot_general(
        pick, flat_back, (((0,), (0,)), ((), ())), preferred_element_type=jnp.float32
    )
    token_grads = jnp.sum(per_assign.reshape(tok, 2, feat), axis=1).astype(jnp.bfloat16)
    gate_assign = lax.dot_general(
        pick,
        back_gate.reshape(experts * cap, 1),
        (((0,), (0,)), ((), ())),
        preferred_element_type=jnp.float32,
    )
    gate_grads = gate_assign.reshape(tok, 2).astype(jnp.bfloat16)
    grad_in_weights = grad_first.astype(jnp.bfloat16)[None]
    grad_out_weights = grad_second.astype(jnp.bfloat16)[None]
    return (token_grads, gate_grads, grad_in_weights, grad_out_weights)


def solution(mesh):
    in_specs = (
        P(("expert", "dp"), None),
        P(("expert", "dp"), None),
        P(("expert", "dp"), None),
        P(("expert", "dp"), None),
        P("expert", None, "dp"),
        P("expert", "dp", None),
    )
    out_specs = (
        P(("expert", "dp"), None),
        P(("expert", "dp"), None),
        P("expert", None, "dp"),
        P("expert", "dp", None),
    )
    sizes = dict(mesh.shape)

    def run(tokens, *rest):
        zs = sizes["dp"]
        row_bytes = 2 * (2 * tokens.shape[1] + LANES)
        small = tokens.shape[0] * row_bytes <= GATHER_BYTES
        cube = sizes["expert"] == 8 and zs > 1 and zs & (zs - 1) == 0
        plan = fused if small and cube else per_device
        return mapped(plan)(tokens, *rest)

    def mapped(plan):
        return jax.shard_map(
            plan, mesh=mesh, in_specs=in_specs, out_specs=out_specs, check_vma=False
        )

    return run
```

```python
import functools
import jax
import jax.numpy as jnp
from jax import lax
from jax.experimental import pallas as pl
from jax.experimental.pallas import tpu as pltpu
from jax.sharding import PartitionSpec as P

LANES = 128
GATHER_BYTES = 8 << 20


def flip(v, bit):
    return v + bit - 2 * bit * ((v // bit) % 2)


def fused_kernel(
    tok, feat, hid, zs, cap, chunks,
    tok_ref, cot_ref, ids_ref, gates_ref, w1_hbm, w2_hbm,
    grads_ref, gate_ref, xr_ref, sc_ref, hid_ref, pg_ref,
    G, W1, W2, CR, BE, TP, RC, S1, A1, A2, A3, S3, ZR,
    wsem, zs_s, zs_r, xs_s, xs_r, ys_s, ys_r, dxs, dxr, dys, dyr, cs_s, cs_r,
    rc_s, rc_r, ra_s, ra_r, rb_s, rb_r, rz_s, rz_r,
):
    f32, bf = jnp.float32, jnp.bfloat16
    e = lax.axis_index("expert")
    z = lax.axis_index("dp")
    experts = G.shape[0] // zs
    c, xb, yb = e % 2, (e // 2) % 2, (e // 4) % 2
    ec, ex, ey, exy = flip(e, 1), flip(e, 2), flip(e, 4), flip(flip(e, 2), 4)
    zp = [z]
    for d in range(1, zs):
        v = z
        for b in range(8):
            if (d >> b) & 1:
                v = flip(v, 1 << b)
        zp.append(v)
    wide = 2 * feat + LANES
    hw = (wide // LANES // 2) * LANES
    blk = lambda ee, j: j * experts + ee

    loads = [
        pltpu.make_async_copy(w1_hbm, W1, wsem.at[0]),
        pltpu.make_async_copy(w2_hbm, W2, wsem.at[1]),
    ]
    for l in loads:
        l.start()
    eye = lax.broadcasted_iota(jnp.int32, (tok, tok), 0) == lax.broadcasted_iota(
        jnp.int32, (tok, tok), 1)
    col = lambda r: jnp.sum(jnp.where(eye, r, 0.0), axis=1, keepdims=True)
    ids_f, gates_f = ids_ref[...].astype(f32), gates_ref[...].astype(f32)
    ln = lax.broadcasted_iota(jnp.int32, (tok, LANES), 1)
    meta = jnp.zeros((tok, LANES), f32)
    for k, r in enumerate((ids_f[0:1], ids_f[1:2], gates_f[0:1], gates_f[1:2])):
        meta = jnp.where(ln == k, col(r), meta)
    G[pl.ds(e, 1), :, 0:feat] = tok_ref[...][None]
    G[pl.ds(e, 1), :, feat:2 * feat] = cot_ref[...][None]
    G[pl.ds(e, 1), :, 2 * feat:] = meta.astype(bf)[None]

    barrier = pltpu.get_barrier_semaphore()
    peers = [(ec, z), (ex, z), (ey, z)] + [(e, zp[d]) for d in range(1, zs)]
    for p in peers:
        pl.semaphore_signal(barrier, inc=1, device_id=p, device_id_type=pl.DeviceIdType.MESH)
    pl.semaphore_wait(barrier, len(peers))

    sends = []

    def go(src, dst, ss, rs, dev):
        cp = pltpu.make_async_remote_copy(
            src_ref=src, dst_ref=dst, send_sem=ss, recv_sem=rs,
            device_id=dev, device_id_type=pl.DeviceIdType.MESH,
        )
        cp.start()
        sends.append(cp)
        return cp

    xc, yc, dx, dy, cc = [], [], [], [], {}
    zc = [None]

    def core_send(b, j, k):
        cc[j, k] = go(G.at[b], G.at[b], cs_s.at[k * zs + j], cs_r.at[k * zs + j], (ec, z))

    def plane(j):
        b = blk(e, j)
        xc.append(go(G.at[b], G.at[b], xs_s.at[j], xs_r.at[j], (ex, z)))
        yc.append(go(G.at[b], G.at[b], ys_s.at[j], ys_r.at[j], (ey, z)))
        core_send(b, j, 0)

    def diag(j):
        bx, by = blk(ex, j), blk(ey, j)
        xc[j].wait_recv()
        v = G.at[bx, :, pl.ds(0, hw)]
        dy.append(go(v, v, dys.at[j], dyr.at[j], (ey, z)))
        core_send(bx, j, 1)
        yc[j].wait_recv()
        v = G.at[by, :, pl.ds(hw, wide - hw)]
        dx.append(go(v, v, dxs.at[j], dxr.at[j], (ex, z)))
        core_send(by, j, 2)

    def finish(j):
        dy[j].wait_recv()
        dx[j].wait_recv()
        core_send(blk(exy, j), j, 3)

    per = G.shape[0] // 2
    zh = zs // 2
    gt, gr = per * tok, per * cap
    ef = e.astype(f32)
    ti = lax.broadcasted_iota(jnp.int32, (gt, gt), 0)
    tj = lax.broadcasted_iota(jnp.int32, (gt, gt), 1)
    lower = jnp.where((ti // tok == tj // tok) & (tj < ti), 1.0, 0.0).astype(bf)
    base = ((lax.broadcasted_iota(jnp.int32, (gt, gr), 0) // tok) * cap).astype(f32)
    lane = lax.broadcasted_iota(jnp.int32, (gt, gr), 1).astype(f32)
    tdims = (((0,), (0,)), ((), ()))
    ndims = (((1,), (1,)), ((), ()))
    picks, metas, gsums = [], [], [None, None]
    step = min(hid, 256)

    def pick_group(g):
        for j in range(g * zh, (g + 1) * zh):
            for k in range(4):
                cc[j, k].wait_recv()
        m = G[g * per:(g + 1) * per, :, 2 * feat:].reshape(gt, LANES).astype(f32)
        m0 = m[:, 0:1] == ef
        m1 = m[:, 1:2] == ef
        mask = jnp.where(m0 | m1, 1.0, 0.0)
        gtok = jnp.where(m0, m[:, 2:3], 0.0) + jnp.where(m1, m[:, 3:4], 0.0)
        slot = jnp.dot(lower, jnp.broadcast_to(mask, (gt, gr)).astype(bf),
                       preferred_element_type=f32)
        pick = jnp.where((slot + base == lane) & (mask > 0.0), 1.0, 0.0).astype(bf)
        picks.append(pick)
        metas.append(m)
        gate = lax.dot_general(pick, jnp.broadcast_to(gtok, (gt, LANES)).astype(bf),
                               tdims, preferred_element_type=f32)
        sl = slice(g * gr, (g + 1) * gr)
        BE[sl, :] = gate
        xg = G[g * per:(g + 1) * per, :, 0:feat].reshape(gt, feat)
        xr_ref[sl, :] = lax.dot_general(pick, xg, tdims, preferred_element_type=f32).astype(bf)
        cg = G[g * per:(g + 1) * per, :, feat:2 * feat].reshape(gt, feat)
        cr = lax.dot_general(pick, cg, tdims, preferred_element_type=f32)
        CR[sl, :] = cr.astype(bf)
        sc_ref[sl, :] = (gate[:, 0:1] * cr).astype(bf)

    def hidden_step(i):
        sl, fs = slice(0, 2 * gr), slice(i * step, (i + 1) * step)
        pre = jnp.dot(xr_ref[sl, :], W1[:, fs], preferred_element_type=f32)
        back = lax.dot_general(CR[sl, :], W2[fs, :], ndims, preferred_element_type=f32)
        cdf = 0.5 * (1.0 + lax.erf(pre * 0.7071067811865476))
        pdf = 0.3989422804014327 * jnp.exp(-0.5 * pre * pre)
        h = (pre * cdf).astype(bf)
        hid_ref[sl, fs] = h
        pg_ref[sl, fs] = (BE[sl, 0:1] * back * (cdf + pre * pdf)).astype(bf)
        t = jnp.sum(h.astype(f32) * back, axis=1, keepdims=True)
        for g in range(2):
            part = t[g * gr:(g + 1) * gr]
            gsums[g] = part if gsums[g] is None else gsums[g] + part

    for d in range(1, zs):
        zc.append(go(G.at[blk(e, 0)], G.at[blk(e, d)], zs_s.at[d], zs_r.at[d], (e, zp[d])))
    for j in range(zs):
        if j:
            zc[j].wait_recv()
        plane(j)
        if j:
            diag(j - 1)
    for j in range(zh):
        finish(j)
    diag(zs - 1)
    for j in range(zh, zs):
        finish(j)
    pick_group(0)
    pick_group(1)
    for l in loads:
        l.wait()
    for i in range(hid // step):
        hidden_step(i)

    def place(i):
        lo, w = chunks[i]
        n = min(lo + w, feat) - lo
        part = lax.dot_general(pg_ref[...], W1[lo:lo + n, :], ndims,
                               preferred_element_type=f32).astype(bf)
        for g in range(2):
            js, rs = slice(g * zh, (g + 1) * zh), slice(g * gr, (g + 1) * gr)
            t = jnp.dot(picks[g], part[rs], preferred_element_type=f32)
            TP[js, :, :, :, :, lo:lo + n] = t.astype(bf).reshape(zh, 2, 2, 2, tok, n)
            if lo + w > feat:
                hi = gsums[g].astype(bf).astype(f32)
                li = lax.broadcasted_iota(jnp.int32, (gr, LANES), 1)
                extra = jnp.where(li < 2, hi, gsums[g] - hi).astype(bf)
                v = jnp.dot(picks[g], extra, preferred_element_type=f32)
                tl = lax.broadcasted_iota(jnp.int32, (gt, LANES), 1)
                m = metas[g]
                own = jnp.where(tl % 2 == 0, m[:, 0:1], m[:, 1:2]) == ef
                v = jnp.where(own & (tl < 4), v, 0.0)
                TP[js, :, :, :, :, feat:] = v.astype(bf).reshape(zh, 2, 2, 2, tok, LANES)
        ds = pl.ds(lo, w)
        swaps.append(go(TP.at[:, :, :, 1 - c, :, ds], RC.at[:, :, :, :, ds],
                        rc_s.at[i], rc_r.at[i], (ec, z)))

    swaps, firsts, seconds, lasts = [], [], [], []

    def after_core(i):
        lo, w = chunks[i]
        ds = pl.ds(lo, w)
        swaps[i].wait_recv()
        s = (TP[:, :, :, pl.ds(c, 1), :, lo:lo + w].reshape(zs, 2, 2, tok, w).astype(f32)
             + RC[:, :, :, :, lo:lo + w].astype(f32))
        S1[:, :, :, :, lo:lo + w] = s.astype(bf)
        if i % 2 == 0:
            src, dev = S1.at[:, :, 1 - xb, :, ds], (ex, z)
        else:
            src, dev = S1.at[:, 1 - yb, :, :, ds], (ey, z)
        firsts.append(go(src, A1.at[:, :, :, ds], ra_s.at[i], ra_r.at[i], dev))

    def after_first(i):
        lo, w = chunks[i]
        ds = pl.ds(lo, w)
        firsts[i].wait_recv()
        if i % 2 == 0:
            mine, other, dev = S1[:, :, pl.ds(xb, 1), :, lo:lo + w], 1 - yb, (ey, z)
        else:
            mine, other, dev = S1[:, pl.ds(yb, 1), :, :, lo:lo + w], 1 - xb, (ex, z)
        A2[:, :, :, lo:lo + w] = (mine.reshape(zs, 2, tok, w).astype(f32)
                                  + A1[:, :, :, lo:lo + w].astype(f32)).astype(bf)
        seconds.append(go(A2.at[:, other, :, ds], A3.at[:, :, ds],
                          rb_s.at[i], rb_r.at[i], dev))

    def after_second(i):
        lo, w = chunks[i]
        ds = pl.ds(lo, w)
        seconds[i].wait_recv()
        own = yb if i % 2 == 0 else xb
        S3[:, :, lo:lo + w] = (A2[:, pl.ds(own, 1), :, lo:lo + w].reshape(zs, tok, w).astype(f32)
                               + A3[:, :, lo:lo + w].astype(f32)).astype(bf)
        lasts.append([go(S3.at[d, :, ds], ZR.at[d - 1, :, ds],
                         rz_s.at[i * zs + d], rz_r.at[i * zs + d], (e, zp[d]))
                      for d in range(1, zs)])

    n = len(chunks)
    for t in range(n + 5):
        for lag, stage in ((0, place), (1, after_core), (3, after_first), (5, after_second)):
            if 0 <= t - lag < n:
                stage(t - lag)
    for i, (lo, w) in enumerate(chunks):
        total = S3[0, :, lo:lo + w].astype(f32)
        for d in range(1, zs):
            lasts[i][d - 1].wait_recv()
            total = total + ZR[d - 1, :, lo:lo + w].astype(f32)
        m = min(lo + w, feat) - lo
        grads_ref[:, lo:lo + m] = total[:, 0:m].astype(bf)
        if m < w:
            row = lambda k: jnp.sum(
                jnp.where(eye, total[:, m + k:m + k + 1] + total[:, m + k + 2:m + k + 3], 0.0),
                axis=0, keepdims=True)
            first = lax.broadcasted_iota(jnp.int32, (2, tok), 0) == 0
            gate_ref[...] = jnp.where(first, row(0), row(1)).astype(bf)
    for s in sends:
        s.wait_send()


def fused(tokens, cotangent, expert_ids, gates, w_in, w_out):
    tok, feat = tokens.shape
    experts, zs = lax.axis_size("expert"), lax.axis_size("dp")
    hid = w_in.shape[2]
    cap = max(2, 4 * tok // experts)
    bf = jnp.bfloat16
    blocks = experts * zs
    rows = blocks * cap
    width = feat + LANES
    tiles = width // LANES
    a, b = tiles // 4, tiles // 2 - tiles // 4
    widths = (a, b, b, tiles - a - 2 * b)
    chunks, at = [], 0
    for w in widths:
        chunks.append((at * LANES, w * LANES))
        at += w
    nc = len(chunks)
    vm = pl.BlockSpec(memory_space=pltpu.VMEM)
    hbm = pl.BlockSpec(memory_space=pl.ANY)
    dma = lambda n: pltpu.SemaphoreType.DMA((n,))
    V = lambda *s: pltpu.VMEM(s, bf)
    sd = jax.ShapeDtypeStruct
    grads, gate, xr, sc, hd, pg = pl.pallas_call(
        functools.partial(fused_kernel, tok, feat, hid, zs, cap, tuple(chunks)),
        out_shape=(
            sd((tok, feat), bf), sd((2, tok), bf), sd((rows, feat), bf),
            sd((rows, feat), bf), sd((rows, hid), bf), sd((rows, hid), bf),
        ),
        in_specs=[vm, vm, vm, vm, hbm, hbm],
        out_specs=(vm,) * 6,
        scratch_shapes=[
            V(blocks, tok, 2 * feat + LANES), V(feat, hid), V(hid, feat), V(rows, feat),
            pltpu.VMEM((rows, LANES), jnp.float32),
            V(zs, 2, 2, 2, tok, width), V(zs, 2, 2, tok, width), V(zs, 2, 2, tok, width),
            V(zs, 2, tok, width), V(zs, 2, tok, width), V(zs, tok, width),
            V(zs, tok, width), V(zs - 1, tok, width),
            dma(2), dma(zs), dma(zs), dma(zs), dma(zs), dma(zs), dma(zs),
            dma(zs), dma(zs), dma(zs), dma(zs), dma(4 * zs), dma(4 * zs),
            dma(nc), dma(nc), dma(nc), dma(nc), dma(nc), dma(nc), dma(nc * zs), dma(nc * zs),
        ],
        compiler_params=pltpu.CompilerParams(
            collective_id=0, has_side_effects=True, vmem_limit_bytes=48 << 20),
        cost_estimate=pl.CostEstimate(
            flops=6 * rows * feat * hid, bytes_accessed=4 * feat * hid, transcendentals=0),
    )(tokens, cotangent, expert_ids.T, gates.T, w_in[0], w_out[0])
    dims = (((0,), (0,)), ((), ()))
    g1 = lax.dot_general(xr, pg, dims, preferred_element_type=jnp.float32).astype(bf)
    g2 = lax.dot_general(hd, sc, dims, preferred_element_type=jnp.float32).astype(bf)
    return grads, gate.T, g1[None], g2[None]


def normal_parts(pre):
    cdf = 0.5 * (1.0 + lax.erf(pre * 0.7071067811865476))
    pdf = 0.3989422804014327 * jnp.exp(-0.5 * pre * pre)
    return (cdf, pdf)


def per_device(tokens, cotangent, expert_ids, gates, w_in, w_out):
    tok = tokens.shape[0]
    feat = tokens.shape[1]
    experts = lax.axis_size("expert")
    cap = max(2, 4 * tok // experts)
    assign = 2 * tok
    ids = expert_ids.reshape(assign)
    onehot = (ids[:, None] == jnp.arange(experts, dtype=jnp.int32)[None, :]).astype(jnp.float32)
    lower = (jnp.arange(assign)[:, None] > jnp.arange(assign)[None, :]).astype(jnp.float32)
    before = jnp.dot(lower, onehot, preferred_element_type=jnp.float32)
    slot = jnp.sum(before * onehot, axis=1).astype(jnp.int32)
    target = ids * cap + slot
    pick = (jnp.arange(experts * cap, dtype=jnp.int32)[:, None] == target[None, :]).astype(
        jnp.bfloat16
    )
    src_in = jnp.repeat(tokens, 2, axis=0)
    src_cot = jnp.repeat(cotangent, 2, axis=0)
    send_in = (
        jnp.dot(pick, src_in, preferred_element_type=jnp.float32)
        .astype(jnp.bfloat16)
        .reshape(experts, cap, feat)
    )
    send_cot = (
        jnp.dot(pick, src_cot, preferred_element_type=jnp.float32)
        .astype(jnp.bfloat16)
        .reshape(experts, cap, feat)
    )
    send_gate = (
        jnp.dot(pick, gates.reshape(assign, 1), preferred_element_type=jnp.float32)
        .astype(jnp.bfloat16)
        .reshape(experts, cap)
    )
    w_first = w_in[0]
    w_second = w_out[0]
    arrived = (
        lax.all_to_all(send_in, "expert", split_axis=0, concat_axis=0, tiled=True),
        lax.all_to_all(send_cot, "expert", split_axis=0, concat_axis=0, tiled=True),
        lax.all_to_all(send_gate, "expert", split_axis=0, concat_axis=0, tiled=True),
    )
    x_blocks = lax.all_gather(arrived[0], "dp", axis=0, tiled=True)
    cot_blocks = lax.all_gather(arrived[1], "dp", axis=0, tiled=True)
    gate_blocks = lax.all_gather(arrived[2], "dp", axis=0, tiled=True)
    count = x_blocks.shape[0] * x_blocks.shape[1]
    x_rows = x_blocks.reshape(count, feat)
    cot_rows = cot_blocks.reshape(count, feat)
    gate_f = gate_blocks.reshape(count, 1).astype(jnp.float32)
    pre = jnp.dot(x_rows, w_first, preferred_element_type=jnp.float32)
    cdf, pdf = normal_parts(pre)
    hidden = (pre * cdf).astype(jnp.bfloat16)
    back = lax.dot_general(
        cot_rows, w_second, (((1,), (1,)), ((), ())), preferred_element_type=jnp.float32
    )
    scaled = (gate_f * cot_rows.astype(jnp.float32)).astype(jnp.bfloat16)
    grad_second = lax.dot_general(
        hidden, scaled, (((0,), (0,)), ((), ())), preferred_element_type=jnp.float32
    )
    pre_grad = (gate_f * back * (cdf + pre * pdf)).astype(jnp.bfloat16)
    grad_first = lax.dot_general(
        x_rows, pre_grad, (((0,), (0,)), ((), ())), preferred_element_type=jnp.float32
    )
    row_part = lax.dot_general(
        pre_grad, w_first, (((1,), (1,)), ((), ())), preferred_element_type=jnp.float32
    ).astype(jnp.bfloat16)
    gate_part = jnp.sum(hidden.astype(jnp.float32) * back, axis=1)
    row_sums = lax.psum_scatter(row_part, "dp", scatter_dimension=0, tiled=True)
    gate_sums = lax.psum_scatter(gate_part, "dp", scatter_dimension=0, tiled=True)
    row_back = row_sums.reshape(experts, cap, feat)
    gate_back = gate_sums.astype(jnp.bfloat16).reshape(experts, cap)
    back_rows, back_gate = (
        lax.all_to_all(row_back, "expert", split_axis=0, concat_axis=0, tiled=True),
        lax.all_to_all(gate_back, "expert", split_axis=0, concat_axis=0, tiled=True),
    )
    flat_back = back_rows.reshape(experts * cap, feat)
    per_assign = lax.dot_general(
        pick, flat_back, (((0,), (0,)), ((), ())), preferred_element_type=jnp.float32
    )
    token_grads = jnp.sum(per_assign.reshape(tok, 2, feat), axis=1).astype(jnp.bfloat16)
    gate_assign = lax.dot_general(
        pick,
        back_gate.reshape(experts * cap, 1),
        (((0,), (0,)), ((), ())),
        preferred_element_type=jnp.float32,
    )
    gate_grads = gate_assign.reshape(tok, 2).astype(jnp.bfloat16)
    grad_in_weights = grad_first.astype(jnp.bfloat16)[None]
    grad_out_weights = grad_second.astype(jnp.bfloat16)[None]
    return (token_grads, gate_grads, grad_in_weights, grad_out_weights)


def solution(mesh):
    in_specs = (
        P(("expert", "dp"), None),
        P(("expert", "dp"), None),
        P(("expert", "dp"), None),
        P(("expert", "dp"), None),
        P("expert", None, "dp"),
        P("expert", "dp", None),
    )
    out_specs = (
        P(("expert", "dp"), None),
        P(("expert", "dp"), None),
        P("expert", None, "dp"),
        P("expert", "dp", None),
    )
    sizes = dict(mesh.shape)

    def run(tokens, *rest):
        zs = sizes["dp"]
        row_bytes = 2 * (2 * tokens.shape[1] + LANES)
        small = tokens.shape[0] * row_bytes <= GATHER_BYTES
        cube = sizes["expert"] == 8 and zs > 1 and zs & (zs - 1) == 0
        plan = fused if small and cube else per_device
        return mapped(plan)(tokens, *rest)

    def mapped(plan):
        return jax.shard_map(
            plan, mesh=mesh, in_specs=in_specs, out_specs=out_specs, check_vma=False
        )

    return run
```
